768 devices in a mesh: node: 48 (over z_lo, y), local: 16 (over x, z_hi, core).
Axes of the slice: x: 4, y: 8, z: 12 (z_hi: 2, z_lo: 6; z = z_hi * 6 + z_lo), core: 2. Of those that a mesh axis runs over, the one named last changes fastest.
Arguments:
- inputs: bfloat16 [98304, 8192], P(('node', 'local')), may hold values from -6 to 6
- key_grad: bfloat16 [98304, 1024], P(('node', 'local')), may hold values from -6 to 6
- weight_codes: bfloat16 [8192, 1024], P('local'), may hold values from -0.1875 to 0.1875
- weight_scales: float32 [64, 1024], P('local'), may hold values from 0.5 to 2
Outputs:
- input_grad: bfloat16 [98304, 8192], P(('node', 'local'))
- weight_grad: float32 [8192, 1024], P('local')
The draws below stay inside these ranges and needn't reach their ends.
All inputs are finite; a program needn't handle non-finite values.
Results may differ from the reference program's by a relative error of at most 0.0049.
Values may be sent and summed in bfloat16 or wider, within the bound.
No kernel may reach another device: no remote copies, remote signals or barrier semaphores. Data moves between devices by JAX's collectives and lax.ppermute only.
A program may use at most 64 MiB of HBM per device.

```python
import math
import jax
import jax.numpy as jnp
from jax import lax

D = 8192
QBLOCK = 128
KV_COLS = 1024
TOKENS = 98304


def level_of(stream_key, shape, pieces, smallest, high):
    def one(dim, parts):
        steps = jax.random.uniform(jax.random.fold_in(jax.random.fold_in(stream_key, 6), dim), (parts,), jnp.float32, smallest / len(pieces), high / len(pieces))
        return jnp.repeat(jnp.exp(steps), shape[dim] // parts).reshape((-1,) + (1,) * (len(shape) - dim - 1))

    level = one(*pieces[0])
    for cut in pieces[1:]:
        level = level * one(*cut)
    return level


def normal_values(own_key, shape, deviation, bound, split=(), held_as=jnp.bfloat16):
    values = deviation * jax.random.normal(own_key, shape, jnp.float32)
    if split:
        values = values * level_of(own_key, shape, split, -0.22, 0.18)
    return jnp.clip(values, -bound, bound).astype(held_as)


def setup_inputs(seed: int = 0) -> dict:
    splits = jax.random.split(jax.random.key(seed), 5)
    inputs = normal_values(splits[0], (TOKENS, D), 1.0, 6.0, ((0, 768),))
    key_grad = normal_values(splits[1], (TOKENS, KV_COLS), 1.0, 6.0, ((0, 768),))
    weight_codes = normal_values(splits[2], (D, KV_COLS), KV_COLS ** -0.5, 0.1875, ((0, 16),))
    weight_scales = jnp.clip(jnp.exp(math.log(2.0) - 1.3862944 * jax.random.uniform(splits[3], (D // QBLOCK, KV_COLS), jnp.float32) ** level_of(splits[3], (D // QBLOCK, KV_COLS), ((0, 16),), -0.2, 0.2)), 0.5, 2.0)
    return {"inputs": inputs, "key_grad": key_grad, "weight_codes": weight_codes, "weight_scales": weight_scales}


def reference(inputs, key_grad, weight_codes, weight_scales):
    scale_rows = weight_scales.shape[0]
    weight = (weight_codes.astype(jnp.float32).reshape(scale_rows, QBLOCK, KV_COLS) * weight_scales[:, None, :]).reshape(D, KV_COLS).astype(jnp.bfloat16)
    input_grad = lax.dot_general(key_grad, weight, (((1,), (1,)), ((), ())), preferred_element_type=jnp.float32).astype(jnp.bfloat16)
    factor = 1.0 / math.sqrt(TOKENS)
    weight_grad = lax.dot_general(inputs, key_grad, (((0,), (0,)), ((), ())), preferred_element_type=jnp.float32) * factor
    return (input_grad, weight_grad)
```

```python
import math

import jax
import jax.numpy as jnp
from jax import lax
from jax.sharding import Mesh
from jax.sharding import PartitionSpec as P

QBLOCK = 128
AXES = ("zt", "zp", "y", "x", "zh", "c")
SIZES = (3, 2, 8, 4, 2, 2)
BF16 = jnp.bfloat16
F32 = jnp.float32


def swapped(value, axis):
    return lax.ppermute(value, axis, [(0, 1), (1, 0)])


def pair_in_order(mine, other, position, axis):
    first = jnp.where(position == 0, mine, other)
    second = jnp.where(position == 0, other, mine)
    return jnp.concatenate([first, second], axis=axis)


def local(inputs, key_grad, weight_codes, weight_scales):
    tokens, width = inputs.shape
    rows, cols = weight_codes.shape
    scale_rows = weight_scales.shape[0]
    zp, y, x, zh, c = (lax.axis_index(a) for a in ("zp", "y", "x", "zh", "c"))
    nx, ny, nt = 4, 8, 3
    half = rows // 2
    piece = half // ny
    total_tokens = tokens * math.prod(SIZES)
    factor = 1.0 / math.sqrt(total_tokens)

    with jax.named_scope("weight"):
        weight = (
            (
                weight_codes.astype(F32).reshape(scale_rows, QBLOCK, cols)
                * weight_scales[:, None, :]
            )
            .reshape(rows, cols)
            .astype(BF16)
        )
        share = rows // ny
        mine = lax.dynamic_slice_in_dim(weight, y * share, share, 0)
        theirs = swapped(mine, "zh")
        weight_other = lax.all_gather(theirs, "y", axis=0, tiled=True)
        weights = pair_in_order(weight, weight_other, zh, 0)

    with jax.named_scope("key_grads"):
        both = pair_in_order(key_grad[None], swapped(key_grad, "zp")[None], zp, 0)
        others = [
            lax.ppermute(both, "x", [(i, i ^ k) for i in range(nx)]) for k in (1, 3, 2)
        ]
        by_distance = [both, others[0], others[2], others[1]]
        slots = []
        for i in range(nx):
            value = by_distance[0]
            for k in range(1, nx):
                value = jnp.where((x ^ i) == k, by_distance[k], value)
            slots.append(value)
        column = jnp.stack(slots, axis=1)
        keys = pair_in_order(column[None], swapped(column, "c")[None], c, 0)

    with jax.named_scope("inputs"):
        sent = inputs.reshape(tokens, nx, 2, 2, 2, half)
        sent = sent.transpose(3, 4, 1, 0, 2, 5).reshape(4 * nx, tokens, 2 * half)
        got = lax.all_to_all(sent, ("c", "zp", "x"), 0, 0, tiled=True)

    with jax.named_scope("input_grad"):
        own = lax.dynamic_index_in_dim(keys, zp, 1, keepdims=False)
        local_part = lax.dot_general(
            own.reshape(2 * nx * tokens, cols),
            weights,
            (((1,), (1,)), ((), ())),
            preferred_element_type=F32,
        ).astype(BF16)
        back = lax.all_to_all(
            local_part.reshape(2 * nx, tokens, 2 * rows), ("c", "x"), 0, 0, tiled=True
        )
        input_grad = (
            back.reshape(2, nx, tokens, 2, rows).transpose(2, 1, 3, 0, 4).reshape(tokens, width)
        )

    with jax.named_scope("weight_grad"):
        partial_value = lax.dot_general(
            got.reshape(4 * nx * tokens, 2 * half),
            keys.reshape(4 * nx * tokens, cols),
            (((0,), (0,)), ((), ())),
            preferred_element_type=F32,
        ) * factor
        chunks = (
            partial_value.reshape(2, ny, piece, cols).transpose(1, 0, 2, 3).astype(BF16)
        )
        total = lax.dynamic_index_in_dim(chunks, y, 0, keepdims=False).astype(F32)
        for k in (4, 3, 5, 2, 6, 1, 7):
            out = lax.dynamic_index_in_dim(chunks, lax.rem(y + k, ny), 0, keepdims=False)
            came = lax.ppermute(out, "y", [(i, (i + k) % ny) for i in range(ny)])
            total = total + came.astype(F32)
        spread = jnp.broadcast_to(total.astype(BF16)[None], (nt, 2, piece, cols))
        spread = lax.all_to_all(
            spread.reshape(nt * 2, piece, cols), ("zt", "zh"), 0, 0, tiled=True
        )
        summed = spread.astype(F32).sum(axis=0).astype(BF16)
        spread = jnp.broadcast_to(summed[None], (2 * ny, piece, cols))
        gathered = lax.all_to_all(spread, ("zp", "y"), 0, 0, tiled=True)
        weight_grad = gathered.reshape(rows, cols).astype(F32)
    return (input_grad, weight_grad)


def solution(mesh):
    fine = Mesh(mesh.devices.reshape(SIZES), AXES)
    tokens_over = P(AXES, None)
    rows_over = P(("x", "zh", "c"), None)
    return jax.shard_map(
        local,
        mesh=fine,
        in_specs=(tokens_over, tokens_over, rows_over, rows_over),
        out_specs=(tokens_over, rows_over),
        check_vma=False,
    )
```

```python
import math

import jax
import jax.numpy as jnp
from jax import lax
from jax.experimental import pallas as pl
from jax.experimental.pallas import tpu as pltpu
from jax.experimental.layout import Layout, with_layout_constraint
from jax.sharding import Mesh
from jax.sharding import PartitionSpec as P

QBLOCK = 128
AXES = ("zt", "zp", "yh", "yl", "x", "zh", "c")
SIZES = (3, 2, 2, 4, 4, 2, 2)
BF16 = jnp.bfloat16
F32 = jnp.float32


def swapped(value, axis):
    return lax.ppermute(value, axis, [(0, 1), (1, 0)])


def around_y(value, distance):
    def target(i):
        return (i + (-distance if distance == 2 and i % 2 else distance)) % 8

    return lax.ppermute(value, ("yh", "yl"), [(i, target(i)) for i in range(8)])


def row_major(value):
    return with_layout_constraint(value, Layout(major_to_minor=tuple(range(value.ndim))))


def pack_kernel(source, target):
    nx, half = 4, target.shape[2] // 2
    for x in range(nx):
        for z in range(2):
            for c in range(2):
                for p in range(2):
                    start = (((x * 2 + z) * 2 + c) * 2 + p) * half
                    slot = (c * 2 + p) * nx + x
                    target[slot, :, z * half : (z + 1) * half] = source[:, start : start + half]


def packed(inputs):
    tokens, width = inputs.shape
    block = tokens // 4
    return pl.pallas_call(
        pack_kernel,
        grid=(tokens // block,),
        out_shape=jax.ShapeDtypeStruct((16, tokens, width // 16), inputs.dtype),
        in_specs=[pl.BlockSpec((block, width), lambda i: (i, 0))],
        out_specs=pl.BlockSpec((16, block, width // 16), lambda i: (0, i, 0)),
        cost_estimate=pl.CostEstimate(
            flops=0, bytes_accessed=4 * tokens * width, transcendentals=0
        ),
    )(inputs)


def pair_in_order(mine, other, position, axis):
    first = jnp.where(position == 0, mine, other)
    second = jnp.where(position == 0, other, mine)
    return jnp.concatenate([first, second], axis=axis)


def local(inputs, key_grad, weight_codes, weight_scales):
    tokens, width = inputs.shape
    rows, cols = weight_codes.shape
    scale_rows = weight_scales.shape[0]
    zp, yh, yl, x, zh, c = (
        lax.axis_index(a) for a in ("zp", "yh", "yl", "x", "zh", "c")
    )
    nx, ny, nt = 4, 8, 3
    half = rows // 2
    piece = half // ny
    y = yh * 4 + yl
    total_tokens = tokens * math.prod(SIZES)
    factor = 1.0 / math.sqrt(total_tokens)

    with jax.named_scope("weight"):
        weight = (
            (
                weight_codes.astype(F32).reshape(scale_rows, QBLOCK, cols)
                * weight_scales[:, None, :]
            )
            .reshape(rows, cols)
            .astype(BF16)
        )
        share = rows // ny
        mine = lax.dynamic_slice_in_dim(weight, y * share, share, 0)

    with jax.named_scope("inputs"):
        theirs = swapped(mine, "zh")
        key_other = swapped(key_grad, "zp")

    with jax.named_scope("key_grads"):
        both = pair_in_order(key_grad[None], key_other[None], zp, 0)
        both, theirs = lax.optimization_barrier((both, theirs))
        shares = pair_in_order(theirs[None], swapped(theirs, "yh")[None], yh, 0)
        from_left = lax.ppermute(both, "x", [(i, (i + 1) % nx) for i in range(nx)])
        from_right = lax.ppermute(both, "x", [(i, (i - 1) % nx) for i in range(nx)])
        opposite = lax.ppermute(from_right, "x", [(i, (i - 1) % nx) for i in range(nx)])
        sent, from_left, opposite, shares = lax.optimization_barrier(
            (packed(inputs), from_left, opposite, shares)
        )
        by_distance = [both, from_right, opposite, from_left]
        slots = []
        for i in range(nx):
            value = by_distance[0]
            for k in range(1, nx):
                value = jnp.where((x + k) % nx == i, by_distance[k], value)
            slots.append(value)
        column = jnp.stack(slots, axis=1)
        keys = pair_in_order(column[None], swapped(column, "c")[None], c, 0)

    with jax.named_scope("inputs"):
        got = row_major(lax.all_to_all(sent, ("c", "zp", "x"), 0, 0, tiled=True))

    with jax.named_scope("input_grad"):
        near = [shares] + [around_y(shares, distance) for distance in (-1, 2, 1)]
        slots = []
        for i in range(4):
            value = near[0]
            for k in (1, 2, 3):
                value = jnp.where((yl + k) % 4 == i, near[k], value)
            slots.append(value)
        weight_other = jnp.stack(slots, axis=1).reshape(rows, cols)
        weights = pair_in_order(weight, weight_other, zh, 0)
        own = lax.dynamic_index_in_dim(keys, zp, 1, keepdims=False)
        local_part = lax.dot_general(
            own.reshape(2 * nx * tokens, cols),
            weights,
            (((1,), (1,)), ((), ())),
            preferred_element_type=F32,
        ).astype(BF16)
        got, local_part = lax.optimization_barrier((got, local_part))
        back = lax.all_to_all(
            local_part.reshape(2 * nx, tokens, 2 * rows), ("c", "x"), 0, 0, tiled=True
        )

    with jax.named_scope("weight_grad"):
        partial_value = lax.dot_general(
            got.reshape(4 * nx * tokens, 2 * half),
            keys.reshape(4 * nx * tokens, cols),
            (((0,), (0,)), ((), ())),
            preferred_element_type=F32,
        ) * factor
        chunks = row_major(partial_value.astype(BF16)).reshape(2, 2, 4, piece, cols)
        total = lax.dynamic_index_in_dim(chunks, yl, 2, keepdims=False).astype(F32)
        for k in (2, 1, 3):
            out = lax.dynamic_index_in_dim(chunks, (yl + k) % 4, 2, keepdims=False)
            total = total + around_y(out, -1 if k == 3 else k).astype(F32)
        kept = lax.dynamic_index_in_dim(total, yh, 1, keepdims=False)
        given = lax.dynamic_index_in_dim(total, 1 - yh, 1, keepdims=False).astype(BF16)
        total = (kept + swapped(given, "yh").astype(F32)).astype(BF16)
        total, back = lax.optimization_barrier((total, back))
        spread = jnp.broadcast_to(total[None], (nt, 2, piece, cols))
        spread = lax.all_to_all(
            spread.reshape(2 * nt, piece, cols), ("zt", "zh"), 0, 0, tiled=True
        )
        summed = spread.astype(F32).sum(axis=0).astype(BF16)
        spread = jnp.broadcast_to(summed[None], (2 * ny, piece, cols))
        gathered = lax.all_to_all(spread, ("zp", "yh", "yl"), 0, 0, tiled=True)
        weight_grad = gathered.reshape(rows, cols).astype(F32)

    with jax.named_scope("input_grad"):
        input_grad = (
            back.reshape(2, nx, tokens, 2, rows).transpose(2, 1, 3, 0, 4).reshape(tokens, width)
        )
    return (input_grad, weight_grad)


def solution(mesh):
    fine = Mesh(mesh.devices.reshape(SIZES), AXES)
    tokens_over = P(AXES, None)
    rows_over = P(("x", "zh", "c"), None)
    return jax.shard_map(
        local,
        mesh=fine,
        in_specs=(tokens_over, tokens_over, rows_over, rows_over),
        out_specs=(tokens_over, rows_over),
        check_vma=False,
    )
```

```python
import math

import jax
import jax.numpy as jnp
from jax import lax
from jax.experimental import pallas as pl
from jax.experimental.pallas import tpu as pltpu
from jax.experimental.layout import Layout, with_layout_constraint
from jax.sharding import Mesh
from jax.sharding import PartitionSpec as P

QBLOCK = 128
AXES = ("zt", "zp", "yh", "yl", "x", "zh", "c")
SIZES = (3, 2, 2, 4, 4, 2, 2)
BF16 = jnp.bfloat16
F32 = jnp.float32


def swapped(value, axis):
    return lax.ppermute(value, axis, [(0, 1), (1, 0)])


def around_y(value, distance):
    def target(i):
        return (i + (-distance if distance == 2 and i % 2 else distance)) % 8

    return lax.ppermute(value, ("yh", "yl"), [(i, target(i)) for i in range(8)])


def row_major(value):
    return with_layout_constraint(value, Layout(major_to_minor=tuple(range(value.ndim))))


def pack_kernel(source, target):
    nx, half = 4, target.shape[2] // 2
    for x in range(nx):
        for z in range(2):
            for c in range(2):
                for p in range(2):
                    start = (((x * 2 + z) * 2 + c) * 2 + p) * half
                    slot = (c * 2 + p) * nx + x
                    target[slot, :, z * half : (z + 1) * half] = source[:, start : start + half]


def packed(inputs):
    tokens, width = inputs.shape
    block = tokens // 4
    return pl.pallas_call(
        pack_kernel,
        grid=(tokens // block,),
        out_shape=jax.ShapeDtypeStruct((16, tokens, width // 16), inputs.dtype),
        in_specs=[pl.BlockSpec((block, width), lambda i: (i, 0))],
        out_specs=pl.BlockSpec((16, block, width // 16), lambda i: (0, i, 0)),
        cost_estimate=pl.CostEstimate(
            flops=0, bytes_accessed=4 * tokens * width, transcendentals=0
        ),
    )(inputs)


def pair_in_order(mine, other, position, axis):
    first = jnp.where(position == 0, mine, other)
    second = jnp.where(position == 0, other, mine)
    return jnp.concatenate([first, second], axis=axis)


def local(inputs, key_grad, weight_codes, weight_scales):
    tokens, width = inputs.shape
    rows, cols = weight_codes.shape
    scale_rows = weight_scales.shape[0]
    zp, yh, yl, x, zh, c = (
        lax.axis_index(a) for a in ("zp", "yh", "yl", "x", "zh", "c")
    )
    nx, ny, nt = 4, 8, 3
    half = rows // 2
    piece = half // ny
    y = yh * 4 + yl
    total_tokens = tokens * math.prod(SIZES)
    factor = 1.0 / math.sqrt(total_tokens)

    with jax.named_scope("weight"):
        weight = (
            (
                weight_codes.astype(F32).reshape(scale_rows, QBLOCK, cols)
                * weight_scales[:, None, :]
            )
            .reshape(rows, cols)
            .astype(BF16)
        )
        share = rows // ny
        mine = lax.dynamic_slice_in_dim(weight, y * share, share, 0)

    with jax.named_scope("inputs"):
        theirs = swapped(mine, "zh")
        key_other = swapped(key_grad, "zp")

    with jax.named_scope("key_grads"):
        both = pair_in_order(key_grad[None], key_other[None], zp, 0)
        shares = pair_in_order(theirs[None], swapped(theirs, "yh")[None], yh, 0)
        from_left = lax.ppermute(both, "x", [(i, (i + 1) % nx) for i in range(nx)])
        from_right = lax.ppermute(both, "x", [(i, (i - 1) % nx) for i in range(nx)])
        opposite = lax.ppermute(from_right, "x", [(i, (i - 1) % nx) for i in range(nx)])
        sent, from_left, opposite, shares = lax.optimization_barrier(
            (packed(inputs), from_left, opposite, shares)
        )
        by_distance = [both, from_right, opposite, from_left]
        slots = []
        for i in range(nx):
            value = by_distance[0]
            for k in range(1, nx):
                value = jnp.where((x + k) % nx == i, by_distance[k], value)
            slots.append(value)
        column = jnp.stack(slots, axis=1)
        keys = pair_in_order(column[None], swapped(column, "c")[None], c, 0)

    with jax.named_scope("inputs"):
        got = row_major(lax.all_to_all(sent, ("c", "zp", "x"), 0, 0, tiled=True))

    with jax.named_scope("input_grad"):
        near = [shares] + [around_y(shares, distance) for distance in (-1, 2, 1)]
        slots = []
        for i in range(4):
            value = near[0]
            for k in (1, 2, 3):
                value = jnp.where((yl + k) % 4 == i, near[k], value)
            slots.append(value)
        weight_other = jnp.stack(slots, axis=1).reshape(rows, cols)
        weights = pair_in_order(weight, weight_other, zh, 0)
        own = lax.dynamic_index_in_dim(keys, zp, 1, keepdims=False)
        local_part = lax.dot_general(
            own.reshape(2 * nx * tokens, cols),
            weights,
            (((1,), (1,)), ((), ())),
            preferred_element_type=F32,
        ).astype(BF16)
        got, local_part = lax.optimization_barrier((got, local_part))
        back = lax.all_to_all(
            local_part.reshape(2 * nx, tokens, 2 * rows), ("c", "x"), 0, 0, tiled=True
        )

    with jax.named_scope("weight_grad"):
        partial_value = lax.dot_general(
            got.reshape(4 * nx * tokens, 2 * half),
            keys.reshape(4 * nx * tokens, cols),
            (((0,), (0,)), ((), ())),
            preferred_element_type=F32,
        ) * factor
        chunks = row_major(partial_value.astype(BF16)).reshape(2, 2, 4, piece, cols)
        total = lax.dynamic_index_in_dim(chunks, yl, 2, keepdims=False).astype(F32)
        for k in (2, 1, 3):
            out = lax.dynamic_index_in_dim(chunks, (yl + k) % 4, 2, keepdims=False)
            total = total + around_y(out, -1 if k == 3 else k).astype(F32)
        kept = lax.dynamic_index_in_dim(total, yh, 1, keepdims=False)
        given = lax.dynamic_index_in_dim(total, 1 - yh, 1, keepdims=False).astype(BF16)
        total = (kept + swapped(given, "yh").astype(F32)).astype(BF16)
        total, back = lax.optimization_barrier((total, back))
        spread = jnp.broadcast_to(total[None], (nt, 2, piece, cols))
        spread = lax.all_to_all(
            spread.reshape(2 * nt, piece, cols), ("zt", "zh"), 0, 0, tiled=True
        )
        summed = spread.astype(F32).sum(axis=0).astype(BF16)
        spread = jnp.broadcast_to(summed[None], (2 * ny, piece, cols))
        gathered = lax.all_to_all(spread, ("zp", "yh", "yl"), 0, 0, tiled=True)
        weight_grad = gathered.reshape(rows, cols).astype(F32)

    with jax.named_scope("input_grad"):
        input_grad = (
            back.reshape(2, nx, tokens, 2, rows).transpose(2, 1, 3, 0, 4).reshape(tokens, width)
        )
    return (input_grad, weight_grad)


def solution(mesh):
    fine = Mesh(mesh.devices.reshape(SIZES), AXES)
    tokens_over = P(AXES, None)
    rows_over = P(("x", "zh", "c"), None)
    return jax.shard_map(
        local,
        mesh=fine,
        in_specs=(tokens_over, tokens_over, rows_over, rows_over),
        out_specs=(tokens_over, rows_over),
        check_vma=False,
    )
```
